32 devices in a mesh: dp: 4 (over y, core), ctx: 8 (over z, x).
Axes of the slice: x: 2, y: 2, z: 4, core: 2. Of those that a mesh axis runs over, the one named last changes fastest.
Arguments:
- tokens: bfloat16 [4, 2048, 1024], P('dp', 'ctx'), may hold values from -6 to 6
- cotangent: bfloat16 [4, 2048, 1024], P('dp', 'ctx'), may hold values from -6 to 6
- segments: int32 [4, 2048], P('dp'), may hold values from 0 to 3, as said below
- span_order: int32 [4, 8], P('dp'), may hold values from 0 to 7, as said below
- query_weight: float32 [1024, 2048], P('dp', 'ctx'), may hold values from -0.1875 to 0.1875
- query_moment: float32 [1024, 2048], P('dp', 'ctx'), may hold values from -27.1529 to 27.1529
- query_second: float32 [1024, 2048], P('dp', 'ctx'), may hold values from 106.496 to 434.176
- key_value_weight: float32 [1024, 2048], P('dp', 'ctx'), may hold values from -0.1875 to 0.1875
- key_value_first_moment: float32 [1024, 2048], P('dp', 'ctx'), may hold values from -36.20387 to 36.20387
- key_value_second_moment: float32 [1024, 2048], P('dp', 'ctx'), may hold values from 212.992 to 860.16
- mixing_weight: float32 [2048, 1024], P('dp', 'ctx'), may hold values from -0.75 to 0.75
- mixing_moment: float32 [2048, 1024], P('dp', 'ctx'), may hold values from -9.050967 to 9.050967
- mixing_second: float32 [2048, 1024], P('dp', 'ctx'), may hold values from 9.8304 to 38.5024
- gate_up_weight: float32 [1024, 6144], P('dp', 'ctx'), may hold values from -0.1875 to 0.1875
- gate_up_moment: float32 [1024, 6144], P('dp', 'ctx'), may hold values from -18.101934 to 18.101934
- gate_up_second: float32 [1024, 6144], P('dp', 'ctx'), may hold values from 38.5024 to 155.648
- down_weight: float32 [3072, 1024], P('dp', 'ctx'), may hold values from -0.109375 to 0.109375
- down_moment: float32 [3072, 1024], P('dp', 'ctx'), may hold values from -36.20387 to 36.20387
- down_second: float32 [3072, 1024], P('dp', 'ctx'), may hold values from 155.648 to 622.592
- norm_gains: float32 [2304], replicated, may hold values from 0.5 to 1.5
- gain_moment: float32 [2304], replicated, may hold values from -72.40774 to 72.40774
- gain_second: float32 [2304], replicated, may hold values from 983.04 to 3850.24
Outputs:
- block_output: bfloat16 [4, 2048, 1024], P('dp', 'ctx')
- input_grad: float32 [4, 2048, 1024], P('dp', 'ctx')
- query_weight_new: float32 [1024, 2048], P('dp', 'ctx')
- query_moment_new: float32 [1024, 2048], P('dp', 'ctx')
- query_second_new: float32 [1024, 2048], P('dp', 'ctx')
- keyval_weight_new: float32 [1024, 2048], P('dp', 'ctx')
- keyval_moment_new: float32 [1024, 2048], P('dp', 'ctx')
- keyval_second_new: float32 [1024, 2048], P('dp', 'ctx')
- mixing_weight_new: float32 [2048, 1024], P('dp', 'ctx')
- mixing_moment_new: float32 [2048, 1024], P('dp', 'ctx')
- mixing_second_new: float32 [2048, 1024], P('dp', 'ctx')
- gate_up_weight_new: float32 [1024, 6144], P('dp', 'ctx')
- gate_up_moment_new: float32 [1024, 6144], P('dp', 'ctx')
- gate_up_second_new: float32 [1024, 6144], P('dp', 'ctx')
- down_weight_new: float32 [3072, 1024], P('dp', 'ctx')
- down_moment_new: float32 [3072, 1024], P('dp', 'ctx')
- down_second_new: float32 [3072, 1024], P('dp', 'ctx')
- norm_gains_new: float32 [2304], replicated
- gain_moment_new: float32 [2304], replicated
- gain_second_new: float32 [2304], replicated
The draws below stay inside these ranges and needn't reach their ends.
Inputs may be any that keep to these rules, and one draw needn't show every extreme that they name: `segments`: read in the order of true positions, a sequence's segment numbers never fall. `span_order`: each row is a permutation of the 8 span numbers; entry c is the span stored in block c of the sequence.
All inputs are finite; a program needn't handle non-finite values.
Results may differ from the reference program's by a relative error of at most 0.024.
Values may be sent and summed in bfloat16 or wider, within the bound.
A program may use at most 320 MiB of HBM per device.

```python
import math
import jax
import jax.numpy as jnp
from jax import lax

MODEL_WIDTH = 1024
QUERY_HEADS = 16
KEY_VALUE_HEADS = 8
HEAD_WIDTH = 128
FF = 3072
SEQUENCE_LENGTH = 2048
SEQ_GRP = 1
STEP = 10
SEQS = 4
SPAN = 256
TOKEN_TOTAL = 8192


cut_count = 3


def order_table(key):
    seq_keys = jax.random.split(key, SEQS)
    return jax.vmap(lambda single: jax.random.permutation(single, SEQUENCE_LENGTH // SPAN))(seq_keys).astype(jnp.int32)


def draw_span_order(key, part):
    return order_table(key)


def draw_segments(key, part):
    orders = order_table(key)
    key = jax.random.fold_in(key, 7)
    spread_key, tail_key, pick_key = jax.random.split(key, 3)
    spread_cuts = jax.random.randint(spread_key, (SEQS, cut_count), 1, SEQUENCE_LENGTH)
    tail_cuts = jax.random.randint(tail_key, (SEQS, cut_count), SEQUENCE_LENGTH - SPAN // 2, SEQUENCE_LENGTH)
    chosen = jax.random.randint(pick_key, (SEQS // SEQ_GRP,), 0, SEQ_GRP)
    member = jnp.arange(SEQS) % SEQ_GRP == jnp.repeat(chosen, SEQ_GRP)
    cuts = jnp.where(member[:, None], tail_cuts, spread_cuts)
    places = jnp.arange(SEQUENCE_LENGTH, dtype=jnp.int32)
    true_segments = jnp.sum((cuts[:, None, :] <= places[None, :, None]).astype(jnp.int32), axis=-1)
    stored = jnp.repeat(orders, SPAN, axis=1) * SPAN + places % SPAN
    return jnp.take_along_axis(true_segments, stored, axis=1).astype(jnp.int32)


def levels(rng, shape, pieces, smallest, top_value):
    factor_of = 1.0
    for dim, shards_of in pieces:
        draws = jax.random.uniform(jax.random.fold_in(jax.random.fold_in(rng, 6), dim), (shards_of,), jnp.float32, smallest / len(pieces), top_value / len(pieces))
        factor_of = factor_of * jnp.repeat(jnp.exp(draws), shape[dim] // shards_of).reshape((-1,) + (1,) * (len(shape) - 1 - dim))
    return factor_of


def noise(rng, shape, width, limit, cuts=(), kind=jnp.bfloat16):
    drawn = width * jax.random.normal(rng, shape, jnp.float32)
    if cuts:
        drawn = drawn * levels(rng, shape, cuts, -0.22, 0.18)
    return jnp.clip(drawn, -limit, limit).astype(kind)


def setup_inputs(seed: int = 0) -> dict:
    arg_keys = jax.random.split(jax.random.key(seed), 23)
    return {
        "tokens": noise(arg_keys[0], (SEQS, SEQUENCE_LENGTH, MODEL_WIDTH), 1.0, 6.0, ((0, 4), (1, 8))),
        "cotangent": noise(arg_keys[1], (SEQS, SEQUENCE_LENGTH, MODEL_WIDTH), 1.0, 6.0, ((0, 4), (1, 8))),
        "segments": draw_segments(jax.random.fold_in(arg_keys[22], 71), 0),
        "span_order": draw_span_order(jax.random.fold_in(arg_keys[22], 71), 0),
        "query_weight": noise(arg_keys[4], (MODEL_WIDTH, QUERY_HEADS * HEAD_WIDTH), MODEL_WIDTH ** -0.5, 0.1875, ((0, 4), (1, 8)), jnp.float32),
        "query_moment": noise(arg_keys[5], (MODEL_WIDTH, QUERY_HEADS * HEAD_WIDTH), (0.055 * TOKEN_TOTAL ** 0.5), 27.1529, ((0, 4), (1, 8)), jnp.float32),
        "query_second": jnp.clip(jnp.exp(math.log(434.176) - 1.40534252 * jax.random.uniform(arg_keys[6], (MODEL_WIDTH, QUERY_HEADS * HEAD_WIDTH), jnp.float32) ** levels(arg_keys[6], (MODEL_WIDTH, QUERY_HEADS * HEAD_WIDTH), ((0, 4), (1, 8)), -0.2, 0.2)), 106.496, 434.176),
        "key_value_weight": noise(arg_keys[7], (MODEL_WIDTH, 2 * KEY_VALUE_HEADS * HEAD_WIDTH), MODEL_WIDTH ** -0.5, 0.1875, ((0, 4), (1, 8)), jnp.float32),
        "key_value_first_moment": noise(arg_keys[8], (MODEL_WIDTH, 2 * KEY_VALUE_HEADS * HEAD_WIDTH), (0.078 * TOKEN_TOTAL ** 0.5), 36.20387, ((0, 4), (1, 8)), jnp.float32),
        "key_value_second_moment": jnp.clip(jnp.exp(math.log(860.16) - 1.3958638 * jax.random.uniform(arg_keys[9], (MODEL_WIDTH, 2 * KEY_VALUE_HEADS * HEAD_WIDTH), jnp.float32) ** levels(arg_keys[9], (MODEL_WIDTH, 2 * KEY_VALUE_HEADS * HEAD_WIDTH), ((0, 4), (1, 8)), -0.2, 0.2)), 212.992, 860.16),
        "mixing_weight": noise(arg_keys[10], (QUERY_HEADS * HEAD_WIDTH, MODEL_WIDTH), (QUERY_HEADS * HEAD_WIDTH // 32) ** -0.5, 0.75, ((0, 4), (1, 8)), jnp.float32),
        "mixing_moment": noise(arg_keys[11], (QUERY_HEADS * HEAD_WIDTH, MODEL_WIDTH), (0.017 * TOKEN_TOTAL ** 0.5), 9.050967, ((0, 4), (1, 8)), jnp.float32),
        "mixing_second": jnp.clip(jnp.exp(math.log(38.5024) - 1.3652409 * jax.random.uniform(arg_keys[12], (QUERY_HEADS * HEAD_WIDTH, MODEL_WIDTH), jnp.float32) ** levels(arg_keys[12], (QUERY_HEADS * HEAD_WIDTH, MODEL_WIDTH), ((0, 4), (1, 8)), -0.2, 0.2)), 9.8304, 38.5024),
        "gate_up_weight": noise(arg_keys[13], (MODEL_WIDTH, 2 * FF), MODEL_WIDTH ** -0.5, 0.1875, ((0, 4), (1, 8)), jnp.float32),
        "gate_up_moment": noise(arg_keys[14], (MODEL_WIDTH, 2 * FF), (0.033 * TOKEN_TOTAL ** 0.5), 18.101934, ((0, 4), (1, 8)), jnp.float32),
        "gate_up_second": jnp.clip(jnp.exp(math.log(155.648) - 1.3968765 * jax.random.uniform(arg_keys[15], (MODEL_WIDTH, 2 * FF), jnp.float32) ** levels(arg_keys[15], (MODEL_WIDTH, 2 * FF), ((0, 4), (1, 8)), -0.2, 0.2)), 38.5024, 155.648),
        "down_weight": noise(arg_keys[16], (FF, MODEL_WIDTH), FF ** -0.5, 0.109375, ((0, 4), (1, 8)), jnp.float32),
        "down_moment": noise(arg_keys[17], (FF, MODEL_WIDTH), (0.066 * TOKEN_TOTAL ** 0.5), 36.20387, ((0, 4), (1, 8)), jnp.float32),
        "down_second": jnp.clip(jnp.exp(math.log(622.592) - 1.3862944 * jax.random.uniform(arg_keys[18], (FF, MODEL_WIDTH), jnp.float32) ** levels(arg_keys[18], (FF, MODEL_WIDTH), ((0, 4), (1, 8)), -0.2, 0.2)), 155.648, 622.592),
        "norm_gains": jnp.clip(1.0 + 0.1 * jax.random.normal(arg_keys[19], (2 * MODEL_WIDTH + 2 * HEAD_WIDTH,), jnp.float32), 0.5, 1.5),
        "gain_moment": noise(arg_keys[20], (2 * MODEL_WIDTH + 2 * HEAD_WIDTH,), (0.15 * TOKEN_TOTAL ** 0.5), 72.40774, (), jnp.float32),
        "gain_second": jnp.clip(jnp.exp(jax.random.uniform(arg_keys[21], (2 * MODEL_WIDTH + 2 * HEAD_WIDTH,), jnp.float32, math.log(983.04), math.log(3850.24))), 983.04, 3850.24),
    }


norm_eps = 1e-06
rope_base = 1000000.0
beta_first = 0.9
beta_second = 0.95
adam_eps = 1e-08
weight_decay = 0.1
gain_rate = 0.4
highest = lax.Precision.HIGHEST

@jax.custom_vjp
def reduced_precision(v):
    return lax.optimization_barrier(v.astype(jnp.bfloat16)).astype(jnp.float32)

@jax.custom_vjp
def low_back(v):
    return v

def low_keep(v):
    return (reduced_precision(v), None)

def low_pass(kept, grad):
    return (grad,)

def back_keep(v):
    return (v, None)

def back_low(kept, grad):
    return (reduced_precision(grad),)
reduced_precision.defvjp(low_keep, low_pass)
low_back.defvjp(back_keep, back_low)

def normalized_input(values, gain):
    return values * lax.rsqrt(lax.optimization_barrier(jnp.mean(values * values, axis=-1, keepdims=True)) + norm_eps) * gain

def rotated_output(values, cosine_table, sine_table):
    half_width = values.shape[-1] // 2
    first_half = values[..., :half_width]
    second_half = values[..., half_width:]
    return jnp.concatenate([first_half * cosine_table - second_half * sine_table, second_half * cosine_table + first_half * sine_table], axis=-1)

def angles_of(positions):
    freq_index = jnp.arange(HEAD_WIDTH // 2, dtype=jnp.float32)
    inverse = rope_base ** (-2.0 * freq_index / HEAD_WIDTH)
    phases = positions.astype(jnp.float32)[..., None] * inverse
    return (jnp.cos(phases), jnp.sin(phases))

def project(left_side, right_side):
    return jnp.dot(left_side, right_side, precision=highest)

def attend_one(query_rows_split, key_rows, value_row_block, permitted_mask):
    sequence_length = query_rows_split.shape[0]
    query_grouped = query_rows_split.reshape(sequence_length, KEY_VALUE_HEADS, QUERY_HEADS // KEY_VALUE_HEADS, HEAD_WIDTH)
    scores = jnp.einsum('qhgd,khd->hgqk', query_grouped, key_rows, precision=highest) * HEAD_WIDTH ** (-0.5)
    scores = low_back(jnp.where(permitted_mask[None, None, :, :], scores, -1e+30))
    weights = reduced_precision(jax.nn.softmax(scores, axis=-1))
    mixed_rows = jnp.einsum('hgqk,khd->qhgd', weights, value_row_block, precision=highest)
    return mixed_rows.reshape(sequence_length, QUERY_HEADS * HEAD_WIDTH)

def layer(params, inputs, cosine_table, sine_table, permitted_mask):
    w_query, w_keyval, w_mixing, w_gateup, w_down, gains = params
    group_width = inputs.shape[0]
    flat_rows = inputs.reshape(-1, MODEL_WIDTH)
    attn_gain = gains[:MODEL_WIDTH]
    mlp_gain = gains[MODEL_WIDTH:2 * MODEL_WIDTH]
    query_gain = gains[2 * MODEL_WIDTH:2 * MODEL_WIDTH + HEAD_WIDTH]
    key_norm_weight = gains[2 * MODEL_WIDTH + HEAD_WIDTH:]
    normed_one = reduced_precision(normalized_input(flat_rows, attn_gain))
    query_raw = low_back(project(normed_one, reduced_precision(w_query)))
    key_value_projected = low_back(project(normed_one, reduced_precision(w_keyval)))
    key_unnormed = key_value_projected[:, :KEY_VALUE_HEADS * HEAD_WIDTH]
    value_row_block = reduced_precision(key_value_projected[:, KEY_VALUE_HEADS * HEAD_WIDTH:])
    query_rotated = reduced_precision(rotated_output(normalized_input(query_raw.reshape(group_width, SEQUENCE_LENGTH, QUERY_HEADS, HEAD_WIDTH), query_gain), cosine_table, sine_table))
    key_rotated = reduced_precision(rotated_output(normalized_input(key_unnormed.reshape(group_width, SEQUENCE_LENGTH, KEY_VALUE_HEADS, HEAD_WIDTH), key_norm_weight), cosine_table, sine_table))
    verified_result = jax.checkpoint(attend_one)
    attention_output = lax.map(lambda packed_tokens: verified_result(packed_tokens[0], packed_tokens[1], packed_tokens[2], packed_tokens[3]), (query_rotated, key_rotated, value_row_block.reshape(group_width, SEQUENCE_LENGTH, KEY_VALUE_HEADS, HEAD_WIDTH), permitted_mask))
    attention_output = reduced_precision(low_back(attention_output.reshape(-1, QUERY_HEADS * HEAD_WIDTH)))
    branch = low_back(project(attention_output, reduced_precision(w_mixing)))
    middle = flat_rows + branch
    normed_two = reduced_precision(normalized_input(middle, mlp_gain))
    gate_up = low_back(project(normed_two, reduced_precision(w_gateup)))
    hidden = reduced_precision(jax.nn.silu(gate_up[:, :FF]) * gate_up[:, FF:])
    result = middle + project(hidden, reduced_precision(w_down))
    return result.reshape(group_width, SEQUENCE_LENGTH, MODEL_WIDTH)

def adamw(weight, moment, second, gradient, rate, decay):
    moment = beta_first * moment + (1.0 - beta_first) * gradient
    second = beta_second * second + (1.0 - beta_second) * gradient * gradient
    scaled = moment / (1.0 - beta_first ** STEP) / (jnp.sqrt(second / (1.0 - beta_second ** STEP)) + adam_eps)
    return (weight - rate * (scaled + decay * weight), moment, second)

def reference(tokens, cotangent, segments, span_order, query_weight, query_moment, query_second, key_value_weight, key_value_first_moment, key_value_second_moment, mixing_weight, mixing_moment, mixing_second, gate_up_weight, gate_up_moment, gate_up_second, down_weight, down_moment, down_second, norm_gains, gain_moment, gain_second):
    offsets = jnp.arange(SEQUENCE_LENGTH, dtype=jnp.int32) % SPAN
    positions = jnp.repeat(span_order, SPAN, axis=1) * SPAN + offsets
    cosine_table, sine_table = angles_of(positions)
    cosine_table = cosine_table[:, :, None, :]
    sine_table = sine_table[:, :, None, :]
    permitted_mask = (segments[:, :, None] == segments[:, None, :]) & (positions[:, None, :] <= positions[:, :, None])
    group_width = 2 if SEQS % 2 == 0 else 1
    group_count = SEQS // group_width
    params = (query_weight, key_value_weight, mixing_weight, gate_up_weight, down_weight, norm_gains)
    inputs = tokens.astype(jnp.float32).reshape(group_count, group_width, SEQUENCE_LENGTH, MODEL_WIDTH)
    backs = cotangent.astype(jnp.float32).reshape(group_count, group_width, SEQUENCE_LENGTH, MODEL_WIDTH)
    cos_groups = cosine_table.reshape(group_count, group_width, SEQUENCE_LENGTH, 1, HEAD_WIDTH // 2)
    sin_groups = sine_table.reshape(group_count, group_width, SEQUENCE_LENGTH, 1, HEAD_WIDTH // 2)
    allowed_groups = permitted_mask.reshape(group_count, group_width, SEQUENCE_LENGTH, SEQUENCE_LENGTH)

    def one_group(totals, packed_tokens):
        group_inputs, cotan_part, cos_part, sin_part, allowed_part = packed_tokens
        outputs, pullback = jax.vjp(lambda weights, values: layer(weights, values, cos_part, sin_part, allowed_part), params, group_inputs)
        weight_grads, group_input_grad = pullback(cotan_part)
        totals = jax.tree.map(lambda earlier, latest: earlier + latest, totals, weight_grads)
        return (totals, (outputs.astype(jnp.bfloat16), group_input_grad))
    zeros = jax.tree.map(jnp.zeros_like, params)
    totals, (outputs, input_grads) = lax.scan(one_group, zeros, (inputs, backs, cos_groups, sin_groups, allowed_groups))
    grad_query, grad_keyval, grad_mixing, grad_gateup, grad_down, grad_gains = totals
    query_new = adamw(query_weight, query_moment, query_second, grad_query, 2.0 / math.sqrt(MODEL_WIDTH), weight_decay)
    keyval_new = adamw(key_value_weight, key_value_first_moment, key_value_second_moment, grad_keyval, 2.0 / math.sqrt(MODEL_WIDTH), weight_decay)
    mixing_new = adamw(mixing_weight, mixing_moment, mixing_second, grad_mixing, 2.0 / math.sqrt(QUERY_HEADS * HEAD_WIDTH // 32), weight_decay)
    gateup_new = adamw(gate_up_weight, gate_up_moment, gate_up_second, grad_gateup, 2.0 / math.sqrt(MODEL_WIDTH), weight_decay)
    down_new = adamw(down_weight, down_moment, down_second, grad_down, 2.0 / math.sqrt(FF), weight_decay)
    gains_new = adamw(norm_gains, gain_moment, gain_second, grad_gains, gain_rate, 0.0)
    return (outputs.reshape(SEQS, SEQUENCE_LENGTH, MODEL_WIDTH), input_grads.reshape(SEQS, SEQUENCE_LENGTH, MODEL_WIDTH), query_new[0], query_new[1], query_new[2], keyval_new[0], keyval_new[1], keyval_new[2], mixing_new[0], mixing_new[1], mixing_new[2], gateup_new[0], gateup_new[1], gateup_new[2], down_new[0], down_new[1], down_new[2], gains_new[0], gains_new[1], gains_new[2])
```

```python
import functools
import math

import jax
import jax.numpy as jnp
from jax import lax
from jax.experimental import pallas as pl
from jax.experimental.pallas import tpu as pltpu
from jax.sharding import PartitionSpec as P

MODEL_WIDTH = 1024
QUERY_HEADS = 16
KEY_VALUE_HEADS = 8
HEAD_WIDTH = 128
FF = 3072
SEQUENCE_LENGTH = 2048
SEQUENCES = 4
STEP = 10


norm_eps = 1e-06
rope_base = 1000000.0
beta_first = 0.9
beta_second = 0.95
adam_eps = 1e-08
weight_decay = 0.1
gain_rate = 0.4


def normalized_input(values, gain):
    return values * lax.rsqrt(jnp.mean(values * values, axis=-1, keepdims=True) + norm_eps) * gain


def rotated_output(values, cosine_table, sine_table):
    half_width = values.shape[-1] // 2
    first_half = values[..., :half_width]
    second_half = values[..., half_width:]
    return jnp.concatenate(
        [
            first_half * cosine_table - second_half * sine_table,
            second_half * cosine_table + first_half * sine_table,
        ],
        axis=-1,
    )


def angles_of(positions):
    freq_index = jnp.arange(HEAD_WIDTH // 2, dtype=jnp.float32)
    inverse = rope_base ** (-2.0 * freq_index / HEAD_WIDTH)
    phases = positions.astype(jnp.float32)[..., None] * inverse
    return (jnp.cos(phases), jnp.sin(phases))


def head_norms(query_raw, key_unnormed, query_gain, key_norm_weight, cosine_table, sine_table):
    query_rotated = rotated_output(
        normalized_input(query_raw, query_gain), cosine_table, sine_table
    )
    key_rotated = rotated_output(
        normalized_input(key_unnormed, key_norm_weight), cosine_table, sine_table
    )
    return (query_rotated, key_rotated)


def swiglu(gate_up):
    return jax.nn.silu(gate_up[:, :FF]) * gate_up[:, FF:]


def adamw(weight, moment, second, gradient, rate, decay):
    moment = beta_first * moment + (1.0 - beta_first) * gradient
    second = beta_second * second + (1.0 - beta_second) * gradient * gradient
    scaled = (
        moment
        / (1.0 - beta_first**STEP)
        / (jnp.sqrt(second / (1.0 - beta_second**STEP)) + adam_eps)
    )
    return (weight - rate * (scaled + decay * weight), moment, second)


def rows_product(left_side, right_side):
    return lax.dot_general(
        left_side, right_side, (((0,), (0,)), ((), ())), preferred_element_type=jnp.float32
    )


def times_transposed(left_side, right_side):
    return lax.dot_general(
        left_side, right_side, (((1,), (1,)), ((), ())), preferred_element_type=jnp.float32
    )


def fetch_forward(query_low, keyval_low, mixing_low, gate_up_low, down_low):
    query_rows, keyval_rows, mixing_rows, gate_up_rows, down_rows = (
        lax.all_gather(query_low, "dp", axis=0, tiled=True),
        lax.all_gather(keyval_low, "dp", axis=0, tiled=True),
        lax.all_gather(mixing_low, "dp", axis=0, tiled=True),
        lax.all_gather(gate_up_low, "dp", axis=0, tiled=True),
        lax.all_gather(down_low, "dp", axis=0, tiled=True),
    )
    return (
        lax.all_gather(query_rows, "ctx", axis=1, tiled=True),
        lax.all_gather(keyval_rows, "ctx", axis=1, tiled=True),
        lax.all_gather(mixing_rows, "ctx", axis=1, tiled=True),
        lax.all_gather(gate_up_rows, "ctx", axis=1, tiled=True),
        lax.all_gather(down_rows, "ctx", axis=1, tiled=True),
    )


def owned(left_rows, right_rows):
    gradient = rows_product(left_rows, right_rows)
    partial_sum = lax.psum_scatter(
        gradient.astype(jnp.bfloat16), "ctx", scatter_dimension=1, tiled=True
    )
    result_shard = lax.psum_scatter(partial_sum, "dp", scatter_dimension=0, tiled=True).astype(
        jnp.float32
    )
    return result_shard


def wide_device(
    tokens,
    cotangent,
    segments,
    span_order,
    query_weight,
    query_moment,
    query_second,
    key_value_weight,
    key_value_first_moment,
    key_value_second_moment,
    mixing_weight,
    mixing_moment,
    mixing_second,
    gate_up_weight,
    gate_up_moment,
    gate_up_second,
    down_weight,
    down_moment,
    down_second,
    norm_gains,
    gain_moment,
    gain_second,
):
    sequence_count = tokens.shape[0]
    span_length = tokens.shape[1]
    count_of_rows = sequence_count * span_length
    ctx_index = lax.axis_index("ctx")
    heads_per_group = QUERY_HEADS // KEY_VALUE_HEADS
    scale_factor = HEAD_WIDTH ** (-0.5)
    query_low_w = query_weight.astype(jnp.bfloat16)
    keyval_low_w = key_value_weight.astype(jnp.bfloat16)
    mixing_low_w = mixing_weight.astype(jnp.bfloat16)
    gate_up_low_w = gate_up_weight.astype(jnp.bfloat16)
    down_low_w = down_weight.astype(jnp.bfloat16)
    query_full, keyval_full, mixing_full, gate_up_full, down_full = fetch_forward(
        query_low_w, keyval_low_w, mixing_low_w, gate_up_low_w, down_low_w
    )
    offsets = jnp.arange(SEQUENCE_LENGTH, dtype=jnp.int32) % span_length
    positions = jnp.repeat(span_order, span_length, axis=1) * span_length + offsets
    own_start = ctx_index * span_length
    own_positions = lax.dynamic_slice_in_dim(positions, own_start, span_length, 1)
    own_segments = lax.dynamic_slice_in_dim(segments, own_start, span_length, 1)
    permitted_mask = (own_segments[:, :, None] == segments[:, None, :]) & (
        positions[:, None, :] <= own_positions[:, :, None]
    )
    permitted_mask = permitted_mask[:, None, None, :, :]
    cosine_table, sine_table = angles_of(own_positions)
    cosine_table = cosine_table[:, :, None, :]
    sine_table = sine_table[:, :, None, :]
    attn_gain = norm_gains[:MODEL_WIDTH]
    mlp_gain = norm_gains[MODEL_WIDTH : 2 * MODEL_WIDTH]
    query_gain = norm_gains[2 * MODEL_WIDTH : 2 * MODEL_WIDTH + HEAD_WIDTH]
    key_norm_weight = norm_gains[2 * MODEL_WIDTH + HEAD_WIDTH :]
    inputs = tokens.astype(jnp.float32).reshape(count_of_rows, MODEL_WIDTH)
    normed_one = normalized_input(inputs, attn_gain).astype(jnp.bfloat16)
    query_raw = jnp.dot(normed_one, query_full, preferred_element_type=jnp.float32).reshape(
        sequence_count, span_length, QUERY_HEADS, HEAD_WIDTH
    )
    key_value_projected = jnp.dot(normed_one, keyval_full, preferred_element_type=jnp.float32)
    key_unnormed = key_value_projected[:, : KEY_VALUE_HEADS * HEAD_WIDTH].reshape(
        sequence_count, span_length, KEY_VALUE_HEADS, HEAD_WIDTH
    )
    value_bfloat = key_value_projected[:, KEY_VALUE_HEADS * HEAD_WIDTH :].astype(jnp.bfloat16)
    head_fn = functools.partial(head_norms, cosine_table=cosine_table, sine_table=sine_table)
    query_rotated, key_rotated = head_fn(query_raw, key_unnormed, query_gain, key_norm_weight)
    query_groups = query_rotated.astype(jnp.bfloat16).reshape(
        sequence_count, span_length, KEY_VALUE_HEADS, heads_per_group, HEAD_WIDTH
    )
    key_bfloat = key_rotated.astype(jnp.bfloat16).reshape(
        sequence_count, span_length, KEY_VALUE_HEADS * HEAD_WIDTH
    )
    gathered_keys, gathered_values = (
        lax.all_gather(key_bfloat, "ctx", axis=1, tiled=True),
        lax.all_gather(
            value_bfloat.reshape(sequence_count, span_length, KEY_VALUE_HEADS * HEAD_WIDTH),
            "ctx",
            axis=1,
            tiled=True,
        ),
    )
    key_head_split = gathered_keys.reshape(
        sequence_count, SEQUENCE_LENGTH, KEY_VALUE_HEADS, HEAD_WIDTH
    )
    value_head_split = gathered_values.reshape(
        sequence_count, SEQUENCE_LENGTH, KEY_VALUE_HEADS, HEAD_WIDTH
    )

    def attention_scores():
        raw_scores = (
            jnp.einsum(
                "sqhgd,skhd->shgqk",
                query_groups,
                key_head_split,
                preferred_element_type=jnp.float32,
            )
            * scale_factor
        )
        return jnp.where(permitted_mask, raw_scores, -1e30)

    scores = attention_scores()
    log_total = jax.nn.logsumexp(scores, axis=-1, keepdims=True)
    probs_low = jnp.exp(scores - log_total).astype(jnp.bfloat16)
    attention_output = jnp.einsum(
        "shgqk,skhd->sqhgd", probs_low, value_head_split, preferred_element_type=jnp.float32
    )
    attended_low = attention_output.reshape(count_of_rows, QUERY_HEADS * HEAD_WIDTH).astype(
        jnp.bfloat16
    )
    middle = inputs + jnp.dot(attended_low, mixing_full, preferred_element_type=jnp.float32)
    normed_two = normalized_input(middle, mlp_gain).astype(jnp.bfloat16)
    gate_up = jnp.dot(normed_two, gate_up_full, preferred_element_type=jnp.float32)
    hidden_low = swiglu(gate_up).astype(jnp.bfloat16)
    result = middle + jnp.dot(hidden_low, down_full, preferred_element_type=jnp.float32)
    block_output = result.astype(jnp.bfloat16).reshape(sequence_count, span_length, MODEL_WIDTH)
    query_back, keyval_back, mixing_back, gate_up_back, down_back = (
        query_full,
        keyval_full,
        mixing_full,
        gate_up_full,
        down_full,
    )
    grad_rows = cotangent.reshape(count_of_rows, MODEL_WIDTH)
    down_new = adamw(
        down_weight,
        down_moment,
        down_second,
        owned(hidden_low, grad_rows),
        2.0 / math.sqrt(FF),
        weight_decay,
    )
    hidden_grad = times_transposed(grad_rows, down_back)
    unused_value, swiglu_back = jax.vjp(swiglu, gate_up)
    gate_up_grad = swiglu_back(hidden_grad)[0].astype(jnp.bfloat16)
    gate_up_new = adamw(
        gate_up_weight,
        gate_up_moment,
        gate_up_second,
        owned(normed_two, gate_up_grad),
        2.0 / math.sqrt(MODEL_WIDTH),
        weight_decay,
    )
    normed_two_grad = times_transposed(gate_up_grad, gate_up_back)
    unused_norm, norm_two_back = jax.vjp(normalized_input, middle, mlp_gain)
    middle_part, mlp_gain_grad = norm_two_back(normed_two_grad)
    middle_grad = grad_rows.astype(jnp.float32) + middle_part
    middle_low = middle_grad.astype(jnp.bfloat16)
    mixing_new = adamw(
        mixing_weight,
        mixing_moment,
        mixing_second,
        owned(attended_low, middle_low),
        2.0 / math.sqrt(QUERY_HEADS * HEAD_WIDTH // 32),
        weight_decay,
    )
    attended_grad = (
        times_transposed(middle_low, mixing_back)
        .astype(jnp.bfloat16)
        .reshape(sequence_count, span_length, KEY_VALUE_HEADS, heads_per_group, HEAD_WIDTH)
    )
    scores = attention_scores()
    probs_full = jnp.exp(scores - log_total)
    probs_again = probs_full.astype(jnp.bfloat16)
    prob_grad = jnp.einsum(
        "sqhgd,skhd->shgqk", attended_grad, value_head_split, preferred_element_type=jnp.float32
    )
    row_delta = jnp.sum(probs_full * prob_grad, axis=-1, keepdims=True)
    score_grad = (probs_full * (prob_grad - row_delta)).astype(jnp.bfloat16)
    query_rot_grad = (
        jnp.einsum(
            "shgqk,skhd->sqhgd", score_grad, key_head_split, preferred_element_type=jnp.float32
        )
        * scale_factor
    )
    key_portion = (
        jnp.einsum(
            "shgqk,sqhgd->skhd", score_grad, query_groups, preferred_element_type=jnp.float32
        )
        * scale_factor
    )
    value_portion = jnp.einsum(
        "shgqk,sqhgd->skhd", probs_again, attended_grad, preferred_element_type=jnp.float32
    )
    key_gradient_total, value_gradient_total = (
        lax.psum_scatter(
            key_portion.reshape(sequence_count, SEQUENCE_LENGTH, KEY_VALUE_HEADS * HEAD_WIDTH),
            "ctx",
            scatter_dimension=1,
            tiled=True,
        ),
        lax.psum_scatter(
            value_portion.reshape(sequence_count, SEQUENCE_LENGTH, KEY_VALUE_HEADS * HEAD_WIDTH),
            "ctx",
            scatter_dimension=1,
            tiled=True,
        ),
    )
    unused_heads, heads_back = jax.vjp(
        head_fn, query_raw, key_unnormed, query_gain, key_norm_weight
    )
    query_raw_grad, key_unnormed_gradient, query_gain_grad, key_gain_grad = heads_back(
        (
            query_rot_grad.reshape(sequence_count, span_length, QUERY_HEADS, HEAD_WIDTH),
            key_gradient_total.reshape(sequence_count, span_length, KEY_VALUE_HEADS, HEAD_WIDTH),
        )
    )
    query_grad = query_raw_grad.reshape(count_of_rows, QUERY_HEADS * HEAD_WIDTH).astype(
        jnp.bfloat16
    )
    keyval_grad = jnp.concatenate(
        [
            key_unnormed_gradient.reshape(count_of_rows, KEY_VALUE_HEADS * HEAD_WIDTH),
            value_gradient_total.reshape(count_of_rows, KEY_VALUE_HEADS * HEAD_WIDTH),
        ],
        axis=1,
    ).astype(jnp.bfloat16)
    query_new = adamw(
        query_weight,
        query_moment,
        query_second,
        owned(normed_one, query_grad),
        2.0 / math.sqrt(MODEL_WIDTH),
        weight_decay,
    )
    keyval_new = adamw(
        key_value_weight,
        key_value_first_moment,
        key_value_second_moment,
        owned(normed_one, keyval_grad),
        2.0 / math.sqrt(MODEL_WIDTH),
        weight_decay,
    )
    normed_one_grad = times_transposed(query_grad, query_back) + times_transposed(
        keyval_grad, keyval_back
    )
    unused_first, norm_one_back = jax.vjp(normalized_input, inputs, attn_gain)
    input_part, attn_gain_grad = norm_one_back(normed_one_grad)
    input_grad = (middle_grad + input_part).reshape(sequence_count, span_length, MODEL_WIDTH)
    gain_terms = jnp.concatenate([attn_gain_grad, mlp_gain_grad, query_gain_grad, key_gain_grad])
    gain_total = lax.psum(gain_terms, ("dp", "ctx"))
    gains_new = adamw(norm_gains, gain_moment, gain_second, gain_total, gain_rate, 0.0)
    return (
        block_output,
        input_grad,
        query_new[0],
        query_new[1],
        query_new[2],
        keyval_new[0],
        keyval_new[1],
        keyval_new[2],
        mixing_new[0],
        mixing_new[1],
        mixing_new[2],
        gate_up_new[0],
        gate_up_new[1],
        gate_up_new[2],
        down_new[0],
        down_new[1],
        down_new[2],
        gains_new[0],
        gains_new[1],
        gains_new[2],
    )


def exchange_pairs(count):
    half = count // 2
    first = [(s, 2 * s) for s in range(half)] + [(half + s, 2 * s + 1) for s in range(half)]
    second = [(s, 2 * s + 1) for s in range(half)] + [(half + s, 2 * s) for s in range(half)]
    return first, second


def pair_columns(shard, ctx_index, count):
    half = shard.shape[1] // 2
    low, high = shard[:, :half], shard[:, half:]
    first, second = exchange_pairs(count)
    is_left = ctx_index < count // 2
    got_first = lax.ppermute(jnp.where(is_left, low, high), "ctx", first)
    got_second = lax.ppermute(jnp.where(is_left, high, low), "ctx", second)
    even = ctx_index % 2 == 0
    return jnp.concatenate(
        [jnp.where(even, got_first, got_second), jnp.where(even, got_second, got_first)], axis=1
    )


def unpair_columns(paired, ctx_index, count):
    half = paired.shape[1] // 2
    left, right = paired[:, :half], paired[:, half:]
    first, second = exchange_pairs(count)
    even = ctx_index % 2 == 0
    got_first = lax.ppermute(jnp.where(even, left, right), "ctx", [(b, a) for a, b in first])
    got_second = lax.ppermute(jnp.where(even, right, left), "ctx", [(b, a) for a, b in second])
    is_left = ctx_index < count // 2
    return jnp.concatenate(
        [jnp.where(is_left, got_first, got_second), jnp.where(is_left, got_second, got_first)],
        axis=1,
    )


def gather(values, axis_name):
    return lax.all_gather(values, axis_name, axis=0, tiled=True)


def scatter(values, axis_name):
    return lax.psum_scatter(
        values.astype(jnp.bfloat16), axis_name, scatter_dimension=0, tiled=True
    ).astype(jnp.float32)


def attend_kernel(order_ref, start_ref, query_ref, key_ref, value_ref, out_ref, sum_ref):
    block = pl.program_id(0)
    blocks = pl.num_programs(0)
    span = query_ref.shape[0]
    width = HEAD_WIDTH
    factor = HEAD_WIDTH ** (-0.5) * math.log2(math.e)
    query = jnp.concatenate([query_ref[:, :width], query_ref[:, width:]], axis=0)
    own = order_ref[block]
    rows = own * span + lax.broadcasted_iota(jnp.int32, (span, span), 0)
    columns = lax.broadcasted_iota(jnp.int32, (span, span), 1)
    starts = start_ref[...]

    def one_span(turn, total):
        place = pl.multiple_of(order_ref[blocks + turn] * span, span)
        scores = lax.dot_general(
            query,
            key_ref[pl.ds(place, span), :],
            (((1,), (1,)), ((), ())),
            preferred_element_type=jnp.float32,
        )
        at = columns + turn * span
        allowed = (at <= rows) & (at >= starts)
        allowed = jnp.concatenate([allowed, allowed], axis=0)
        terms = jnp.where(allowed, jnp.exp2(scores * factor), 0.0).astype(jnp.bfloat16)
        return total + jnp.dot(
            terms, value_ref[pl.ds(place, span), :], preferred_element_type=jnp.float32
        )

    total = lax.fori_loop(
        order_ref[2 * blocks + block],
        own + 1,
        one_span,
        jnp.zeros((2 * span, 2 * width), jnp.float32),
    )
    mixed = total[:, :width] / total[:, width:]
    out_ref[:, :width] = mixed[:span]
    out_ref[:, width:] = mixed[span:]
    sums = jnp.log2(total[:, width:])
    sum_ref[:, :width] = sums[:span]
    sum_ref[:, width:] = sums[span:]


def attention_forward(query, key, value, order_table, starts):
    length, wide = query.shape
    blocks = order_table.shape[0] // 3
    span = length // blocks
    padded = jnp.concatenate([value, jnp.ones_like(value)], axis=1)
    out, sums = pl.pallas_call(
        attend_kernel,
        grid=(blocks,),
        in_specs=[
            pl.BlockSpec(memory_space=pltpu.SMEM),
            pl.BlockSpec((span, 1), lambda i: (i, 0)),
            pl.BlockSpec((span, wide), lambda i: (i, 0)),
            pl.BlockSpec((length, HEAD_WIDTH), lambda i: (0, 0)),
            pl.BlockSpec((length, 2 * HEAD_WIDTH), lambda i: (0, 0)),
        ],
        out_specs=[
            pl.BlockSpec((span, wide), lambda i: (i, 0)),
            pl.BlockSpec((span, wide), lambda i: (i, 0)),
        ],
        out_shape=[
            jax.ShapeDtypeStruct((length, wide), jnp.float32),
            jax.ShapeDtypeStruct((length, wide), jnp.float32),
        ],
        compiler_params=pltpu.CompilerParams(vmem_limit_bytes=40 * 1024 * 1024),
        cost_estimate=pl.CostEstimate(
            flops=4 * length * length * wide // 2,
            bytes_accessed=12 * length * wide,
            transcendentals=length * length,
        ),
        name="attend",
    )(order_table, starts[:, None], query, key, padded)
    return out, sums[:, ::HEAD_WIDTH]


def attend_back_kernel(
    order_ref,
    start_ref,
    sum_ref,
    delta_ref,
    query_ref,
    grad_ref,
    key_ref,
    value_ref,
    query_grad_ref,
    key_grad_ref,
    value_grad_ref,
):
    block = pl.program_id(0)
    blocks = pl.num_programs(0)
    span = query_ref.shape[0]
    width = HEAD_WIDTH
    scale_factor = HEAD_WIDTH ** (-0.5)
    factor = scale_factor * math.log2(math.e)

    @pl.when(block == 0)
    def _():
        key_grad_ref[...] = jnp.zeros_like(key_grad_ref)
        value_grad_ref[...] = jnp.zeros_like(value_grad_ref)

    query = jnp.concatenate([query_ref[:, :width], query_ref[:, width:]], axis=0)
    grad = jnp.concatenate([grad_ref[:, :width], grad_ref[:, width:]], axis=0)
    own = order_ref[block]
    rows = own * span + lax.broadcasted_iota(jnp.int32, (span, span), 1)
    columns = lax.broadcasted_iota(jnp.int32, (span, span), 0)
    starts = start_ref[0]
    sums = sum_ref[0]
    delta = delta_ref[0]

    def one_span(turn, total):
        place = pl.multiple_of(order_ref[blocks + turn] * span, span)
        here = pl.ds(place, span)
        keys = key_ref[here, :]
        scores = lax.dot_general(
            keys, query, (((1,), (1,)), ((), ())), preferred_element_type=jnp.float32
        )
        prob_grad = lax.dot_general(
            value_ref[here, :], grad, (((1,), (1,)), ((), ())), preferred_element_type=jnp.float32
        )
        at = columns + turn * span
        allowed = (at <= rows) & (at >= starts)
        allowed = jnp.concatenate([allowed, allowed], axis=1)
        probs = jnp.where(allowed, jnp.exp2(scores * factor - sums), 0.0)
        score_grad = (probs * (prob_grad - delta)).astype(jnp.bfloat16)
        value_grad_ref[here, :] += jnp.dot(
            probs.astype(jnp.bfloat16), grad, preferred_element_type=jnp.float32
        )
        key_grad_ref[here, :] += (
            jnp.dot(score_grad, query, preferred_element_type=jnp.float32) * scale_factor
        )
        return total + lax.dot_general(
            score_grad, keys, (((0,), (0,)), ((), ())), preferred_element_type=jnp.float32
        )

    total = lax.fori_loop(
        order_ref[2 * blocks + block],
        own + 1,
        one_span,
        jnp.zeros((2 * span, width), jnp.float32),
    )
    total = total * scale_factor
    query_grad_ref[:, :width] = total[:span]
    query_grad_ref[:, width:] = total[span:]


def attention_backward(query, key, value, order_table, starts, sums, attended, attended_grad):
    length, wide = query.shape
    blocks = order_table.shape[0] // 3
    span = length // blocks
    heads = wide // HEAD_WIDTH
    delta = jnp.sum(
        (attended * attended_grad.astype(jnp.float32)).reshape(length, heads, HEAD_WIDTH), axis=-1
    )

    def along_lanes(columns):
        split = columns.reshape(blocks, span, heads)
        return split.transpose(0, 2, 1).reshape(blocks, 1, heads * span)

    by_block = pl.BlockSpec((span, wide), lambda i: (i, 0))
    whole = pl.BlockSpec((length, HEAD_WIDTH), lambda i: (0, 0))
    lane_row = pl.BlockSpec((1, 1, heads * span), lambda i: (i, 0, 0))
    return pl.pallas_call(
        attend_back_kernel,
        grid=(blocks,),
        in_specs=[
            pl.BlockSpec(memory_space=pltpu.SMEM),
            pl.BlockSpec((1, 1, span), lambda i: (i, 0, 0)),
            lane_row,
            lane_row,
            by_block,
            by_block,
            whole,
            whole,
        ],
        out_specs=[by_block, whole, whole],
        out_shape=[
            jax.ShapeDtypeStruct((length, wide), jnp.float32),
            jax.ShapeDtypeStruct((length, HEAD_WIDTH), jnp.float32),
            jax.ShapeDtypeStruct((length, HEAD_WIDTH), jnp.float32),
        ],
        compiler_params=pltpu.CompilerParams(vmem_limit_bytes=40 * 1024 * 1024),
        cost_estimate=pl.CostEstimate(
            flops=10 * length * length * wide // 2,
            bytes_accessed=16 * length * wide,
            transcendentals=length * length,
        ),
        name="attend_back",
    )(
        order_table,
        starts.reshape(blocks, 1, span),
        along_lanes(sums),
        along_lanes(delta),
        query,
        attended_grad,
        key,
        value,
    )


def span_table(segments, span_order, span_length):
    starts = jnp.sum((segments[None, :] < segments[:, None]).astype(jnp.int32), axis=1)
    blocks = span_order.shape[0]
    block_of = jnp.sum(
        jnp.where(
            span_order[None, :] == jnp.arange(blocks, dtype=jnp.int32)[:, None],
            jnp.arange(blocks, dtype=jnp.int32)[None, :],
            0,
        ),
        axis=1,
    )
    first = jnp.min(starts.reshape(blocks, span_length), axis=1) // span_length
    return starts, jnp.concatenate([span_order, block_of, first]).astype(jnp.int32)


def head_device(
    tokens,
    cotangent,
    segments,
    span_order,
    query_weight,
    query_moment,
    query_second,
    key_value_weight,
    key_value_first_moment,
    key_value_second_moment,
    mixing_weight,
    mixing_moment,
    mixing_second,
    gate_up_weight,
    gate_up_moment,
    gate_up_second,
    down_weight,
    down_moment,
    down_second,
    norm_gains,
    gain_moment,
    gain_second,
):
    span_length = tokens.shape[1]
    count = KEY_VALUE_HEADS
    group = QUERY_HEADS // KEY_VALUE_HEADS
    wide = group * HEAD_WIDTH
    ctx_index = lax.axis_index("ctx")
    attn_gain = norm_gains[:MODEL_WIDTH]
    mlp_gain = norm_gains[MODEL_WIDTH : 2 * MODEL_WIDTH]
    query_gain = norm_gains[2 * MODEL_WIDTH : 2 * MODEL_WIDTH + HEAD_WIDTH]
    key_norm_weight = norm_gains[2 * MODEL_WIDTH + HEAD_WIDTH :]

    tokens_full = gather(tokens[0], "ctx")
    keyval_pair = pair_columns(key_value_weight.astype(jnp.bfloat16), ctx_index, count)
    qkv_weight = gather(
        jnp.concatenate([query_weight.astype(jnp.bfloat16), keyval_pair], axis=1), "dp"
    )
    mixing_cols = gather(mixing_weight.astype(jnp.bfloat16), "dp")
    mixing_rows = lax.all_to_all(mixing_cols, "ctx", 0, 1, tiled=True)
    gate_up_cols = gather(
        pair_columns(gate_up_weight.astype(jnp.bfloat16), ctx_index, count), "dp"
    )
    down_cols = gather(down_weight.astype(jnp.bfloat16), "dp")
    down_rows = lax.all_to_all(down_cols, "ctx", 0, 1, tiled=True)
    cotangent_full = gather(cotangent[0], "ctx")

    offsets = jnp.arange(SEQUENCE_LENGTH, dtype=jnp.int32) % span_length
    positions = jnp.repeat(span_order[0], span_length) * span_length + offsets
    cosine_table, sine_table = angles_of(positions)
    head_fn = functools.partial(
        head_norms, cosine_table=cosine_table[:, None, :], sine_table=sine_table[:, None, :]
    )

    normed_one = normalized_input(tokens_full.astype(jnp.float32), attn_gain).astype(jnp.bfloat16)
    qkv = jnp.dot(normed_one, qkv_weight, preferred_element_type=jnp.float32)
    query_raw = qkv[:, :wide].reshape(SEQUENCE_LENGTH, group, HEAD_WIDTH)
    key_raw = qkv[:, wide : wide + HEAD_WIDTH].reshape(SEQUENCE_LENGTH, 1, HEAD_WIDTH)
    value = qkv[:, wide + HEAD_WIDTH :].astype(jnp.bfloat16)
    (query_rot, key_rot), heads_back = jax.vjp(
        head_fn, query_raw, key_raw, query_gain, key_norm_weight
    )
    query_rot = query_rot.astype(jnp.bfloat16).reshape(SEQUENCE_LENGTH, wide)
    key_rot = key_rot[:, 0].astype(jnp.bfloat16)
    starts, order_table = span_table(segments[0], span_order[0], span_length)
    attended_wide, sums = attention_forward(query_rot, key_rot, value, order_table, starts)
    attended = attended_wide.astype(jnp.bfloat16)

    inputs = tokens[0].astype(jnp.float32)
    middle = inputs + scatter(
        jnp.dot(attended, mixing_rows, preferred_element_type=jnp.float32), "ctx"
    )
    normed_two = normalized_input(middle, mlp_gain).astype(jnp.bfloat16)
    normed_two_full = gather(normed_two, "ctx")
    gate_up = jnp.dot(normed_two_full, gate_up_cols, preferred_element_type=jnp.float32)
    half = gate_up.shape[1] // 2

    def gated(both):
        return jax.nn.silu(both[:, :half]) * both[:, half:]

    hidden, gated_back = jax.vjp(gated, gate_up)
    hidden = hidden.astype(jnp.bfloat16)
    hidden_grad = times_transposed(cotangent_full, down_rows)
    gate_up_grad = gated_back(hidden_grad)[0].astype(jnp.bfloat16)
    normed_two_grad = scatter(times_transposed(gate_up_grad, gate_up_cols), "ctx")
    result = middle + scatter(
        jnp.dot(hidden, down_rows, preferred_element_type=jnp.float32), "ctx"
    )
    block_output = result.astype(jnp.bfloat16)[None]

    unused_norm, norm_two_back = jax.vjp(normalized_input, middle, mlp_gain)
    middle_part, mlp_gain_grad = norm_two_back(normed_two_grad)
    middle_grad = cotangent[0].astype(jnp.float32) + middle_part
    middle_low = gather(middle_grad.astype(jnp.bfloat16), "ctx")
    attended_grad = times_transposed(middle_low, mixing_rows).astype(jnp.bfloat16)

    def rows_back(gradient):
        columns = lax.all_to_all(gradient.astype(jnp.bfloat16), "ctx", 1, 0, tiled=True)
        return scatter(columns, "dp")

    down_total = rows_back(rows_product(hidden, cotangent_full))
    gate_up_total = unpair_columns(
        scatter(rows_product(normed_two_full, gate_up_grad), "dp").astype(jnp.bfloat16),
        ctx_index,
        count,
    ).astype(jnp.float32)
    mixing_total = rows_back(rows_product(attended, middle_low))

    query_rot_grad, key_rot_grad, value_grad = attention_backward(
        query_rot, key_rot, value, order_table, starts, sums, attended_wide, attended_grad
    )
    query_raw_grad, key_raw_grad, query_gain_grad, key_gain_grad = heads_back(
        (
            query_rot_grad.reshape(SEQUENCE_LENGTH, group, HEAD_WIDTH),
            key_rot_grad[:, None, :],
        )
    )
    qkv_grad = jnp.concatenate(
        [query_raw_grad.reshape(SEQUENCE_LENGTH, wide), key_raw_grad[:, 0], value_grad], axis=1
    ).astype(jnp.bfloat16)
    normed_one_grad = scatter(times_transposed(qkv_grad, qkv_weight), "ctx")
    qkv_total = scatter(rows_product(normed_one, qkv_grad), "dp").astype(jnp.bfloat16)
    query_total = qkv_total[:, :wide].astype(jnp.float32)
    keyval_total = unpair_columns(qkv_total[:, wide:], ctx_index, count).astype(jnp.float32)
    unused_first, norm_one_back = jax.vjp(normalized_input, inputs, attn_gain)
    input_part, attn_gain_grad = norm_one_back(normed_one_grad)
    input_grad = (middle_grad + input_part)[None]

    gain_terms = jnp.concatenate([attn_gain_grad, mlp_gain_grad, query_gain_grad, key_gain_grad])
    gain_total = lax.psum(gain_terms, ("dp", "ctx"))
    model_rate = 2.0 / math.sqrt(MODEL_WIDTH)
    mixing_rate = 2.0 / math.sqrt(QUERY_HEADS * HEAD_WIDTH // 32)
    down_rate = 2.0 / math.sqrt(FF)
    return (
        block_output,
        input_grad,
        *adamw(query_weight, query_moment, query_second, query_total, model_rate, weight_decay),
        *adamw(
            key_value_weight,
            key_value_first_moment,
            key_value_second_moment,
            keyval_total,
            model_rate,
            weight_decay,
        ),
        *adamw(
            mixing_weight, mixing_moment, mixing_second, mixing_total, mixing_rate, weight_decay
        ),
        *adamw(
            gate_up_weight, gate_up_moment, gate_up_second, gate_up_total, model_rate, weight_decay
        ),
        *adamw(down_weight, down_moment, down_second, down_total, down_rate, weight_decay),
        *adamw(norm_gains, gain_moment, gain_second, gain_total, gain_rate, 0.0),
    )


def solution(mesh):
    in_specs = (
        P("dp", "ctx", None),
        P("dp", "ctx", None),
        P("dp", None),
        P("dp", None),
        P("dp", "ctx"),
        P("dp", "ctx"),
        P("dp", "ctx"),
        P("dp", "ctx"),
        P("dp", "ctx"),
        P("dp", "ctx"),
        P("dp", "ctx"),
        P("dp", "ctx"),
        P("dp", "ctx"),
        P("dp", "ctx"),
        P("dp", "ctx"),
        P("dp", "ctx"),
        P("dp", "ctx"),
        P("dp", "ctx"),
        P("dp", "ctx"),
        P(),
        P(),
        P(),
    )
    out_specs = (
        P("dp", "ctx", None),
        P("dp", "ctx", None),
        P("dp", "ctx"),
        P("dp", "ctx"),
        P("dp", "ctx"),
        P("dp", "ctx"),
        P("dp", "ctx"),
        P("dp", "ctx"),
        P("dp", "ctx"),
        P("dp", "ctx"),
        P("dp", "ctx"),
        P("dp", "ctx"),
        P("dp", "ctx"),
        P("dp", "ctx"),
        P("dp", "ctx"),
        P("dp", "ctx"),
        P("dp", "ctx"),
        P(),
        P(),
        P(),
    )
    fits = mesh.shape["ctx"] == KEY_VALUE_HEADS and mesh.shape["dp"] == SEQUENCES
    per_device = head_device if fits else wide_device
    return jax.shard_map(
        per_device, mesh=mesh, in_specs=in_specs, out_specs=out_specs, check_vma=False
    )
```

```python
import functools
import math

import jax
import jax.numpy as jnp
from jax import lax
from jax.experimental import pallas as pl
from jax.experimental.pallas import tpu as pltpu
from jax.sharding import PartitionSpec as P

MODEL_WIDTH = 1024
QUERY_HEADS = 16
KEY_VALUE_HEADS = 8
HEAD_WIDTH = 128
FF = 3072
SEQUENCE_LENGTH = 2048
SEQUENCES = 4
STEP = 10


norm_eps = 1e-06
rope_base = 1000000.0
beta_first = 0.9
beta_second = 0.95
adam_eps = 1e-08
weight_decay = 0.1
gain_rate = 0.4


def normalized_input(values, gain):
    return values * lax.rsqrt(jnp.mean(values * values, axis=-1, keepdims=True) + norm_eps) * gain


def rotated_output(values, cosine_table, sine_table):
    half_width = values.shape[-1] // 2
    first_half = values[..., :half_width]
    second_half = values[..., half_width:]
    return jnp.concatenate(
        [
            first_half * cosine_table - second_half * sine_table,
            second_half * cosine_table + first_half * sine_table,
        ],
        axis=-1,
    )


def angles_of(positions):
    freq_index = jnp.arange(HEAD_WIDTH // 2, dtype=jnp.float32)
    inverse = rope_base ** (-2.0 * freq_index / HEAD_WIDTH)
    phases = positions.astype(jnp.float32)[..., None] * inverse
    return (jnp.cos(phases), jnp.sin(phases))


def head_norms(query_raw, key_unnormed, query_gain, key_norm_weight, cosine_table, sine_table):
    query_rotated = rotated_output(
        normalized_input(query_raw, query_gain), cosine_table, sine_table
    )
    key_rotated = rotated_output(
        normalized_input(key_unnormed, key_norm_weight), cosine_table, sine_table
    )
    return (query_rotated, key_rotated)


def swiglu(gate_up):
    return jax.nn.silu(gate_up[:, :FF]) * gate_up[:, FF:]


def adamw(weight, moment, second, gradient, rate, decay):
    moment = beta_first * moment + (1.0 - beta_first) * gradient
    second = beta_second * second + (1.0 - beta_second) * gradient * gradient
    scaled = (
        moment
        / (1.0 - beta_first**STEP)
        / (jnp.sqrt(second / (1.0 - beta_second**STEP)) + adam_eps)
    )
    return (weight - rate * (scaled + decay * weight), moment, second)


def rows_product(left_side, right_side):
    return lax.dot_general(
        left_side, right_side, (((0,), (0,)), ((), ())), preferred_element_type=jnp.float32
    )


def times_transposed(left_side, right_side):
    return lax.dot_general(
        left_side, right_side, (((1,), (1,)), ((), ())), preferred_element_type=jnp.float32
    )


def fetch_forward(query_low, keyval_low, mixing_low, gate_up_low, down_low):
    query_rows, keyval_rows, mixing_rows, gate_up_rows, down_rows = (
        lax.all_gather(query_low, "dp", axis=0, tiled=True),
        lax.all_gather(keyval_low, "dp", axis=0, tiled=True),
        lax.all_gather(mixing_low, "dp", axis=0, tiled=True),
        lax.all_gather(gate_up_low, "dp", axis=0, tiled=True),
        lax.all_gather(down_low, "dp", axis=0, tiled=True),
    )
    return (
        lax.all_gather(query_rows, "ctx", axis=1, tiled=True),
        lax.all_gather(keyval_rows, "ctx", axis=1, tiled=True),
        lax.all_gather(mixing_rows, "ctx", axis=1, tiled=True),
        lax.all_gather(gate_up_rows, "ctx", axis=1, tiled=True),
        lax.all_gather(down_rows, "ctx", axis=1, tiled=True),
    )


def owned(left_rows, right_rows):
    gradient = rows_product(left_rows, right_rows)
    partial_sum = lax.psum_scatter(
        gradient.astype(jnp.bfloat16), "ctx", scatter_dimension=1, tiled=True
    )
    result_shard = lax.psum_scatter(partial_sum, "dp", scatter_dimension=0, tiled=True).astype(
        jnp.float32
    )
    return result_shard


def wide_device(
    tokens,
    cotangent,
    segments,
    span_order,
    query_weight,
    query_moment,
    query_second,
    key_value_weight,
    key_value_first_moment,
    key_value_second_moment,
    mixing_weight,
    mixing_moment,
    mixing_second,
    gate_up_weight,
    gate_up_moment,
    gate_up_second,
    down_weight,
    down_moment,
    down_second,
    norm_gains,
    gain_moment,
    gain_second,
):
    sequence_count = tokens.shape[0]
    span_length = tokens.shape[1]
    count_of_rows = sequence_count * span_length
    ctx_index = lax.axis_index("ctx")
    heads_per_group = QUERY_HEADS // KEY_VALUE_HEADS
    scale_factor = HEAD_WIDTH ** (-0.5)
    query_low_w = query_weight.astype(jnp.bfloat16)
    keyval_low_w = key_value_weight.astype(jnp.bfloat16)
    mixing_low_w = mixing_weight.astype(jnp.bfloat16)
    gate_up_low_w = gate_up_weight.astype(jnp.bfloat16)
    down_low_w = down_weight.astype(jnp.bfloat16)
    query_full, keyval_full, mixing_full, gate_up_full, down_full = fetch_forward(
        query_low_w, keyval_low_w, mixing_low_w, gate_up_low_w, down_low_w
    )
    offsets = jnp.arange(SEQUENCE_LENGTH, dtype=jnp.int32) % span_length
    positions = jnp.repeat(span_order, span_length, axis=1) * span_length + offsets
    own_start = ctx_index * span_length
    own_positions = lax.dynamic_slice_in_dim(positions, own_start, span_length, 1)
    own_segments = lax.dynamic_slice_in_dim(segments, own_start, span_length, 1)
    permitted_mask = (own_segments[:, :, None] == segments[:, None, :]) & (
        positions[:, None, :] <= own_positions[:, :, None]
    )
    permitted_mask = permitted_mask[:, None, None, :, :]
    cosine_table, sine_table = angles_of(own_positions)
    cosine_table = cosine_table[:, :, None, :]
    sine_table = sine_table[:, :, None, :]
    attn_gain = norm_gains[:MODEL_WIDTH]
    mlp_gain = norm_gains[MODEL_WIDTH : 2 * MODEL_WIDTH]
    query_gain = norm_gains[2 * MODEL_WIDTH : 2 * MODEL_WIDTH + HEAD_WIDTH]
    key_norm_weight = norm_gains[2 * MODEL_WIDTH + HEAD_WIDTH :]
    inputs = tokens.astype(jnp.float32).reshape(count_of_rows, MODEL_WIDTH)
    normed_one = normalized_input(inputs, attn_gain).astype(jnp.bfloat16)
    query_raw = jnp.dot(normed_one, query_full, preferred_element_type=jnp.float32).reshape(
        sequence_count, span_length, QUERY_HEADS, HEAD_WIDTH
    )
    key_value_projected = jnp.dot(normed_one, keyval_full, preferred_element_type=jnp.float32)
    key_unnormed = key_value_projected[:, : KEY_VALUE_HEADS * HEAD_WIDTH].reshape(
        sequence_count, span_length, KEY_VALUE_HEADS, HEAD_WIDTH
    )
    value_bfloat = key_value_projected[:, KEY_VALUE_HEADS * HEAD_WIDTH :].astype(jnp.bfloat16)
    head_fn = functools.partial(head_norms, cosine_table=cosine_table, sine_table=sine_table)
    query_rotated, key_rotated = head_fn(query_raw, key_unnormed, query_gain, key_norm_weight)
    query_groups = query_rotated.astype(jnp.bfloat16).reshape(
        sequence_count, span_length, KEY_VALUE_HEADS, heads_per_group, HEAD_WIDTH
    )
    key_bfloat = key_rotated.astype(jnp.bfloat16).reshape(
        sequence_count, span_length, KEY_VALUE_HEADS * HEAD_WIDTH
    )
    gathered_keys, gathered_values = (
        lax.all_gather(key_bfloat, "ctx", axis=1, tiled=True),
        lax.all_gather(
            value_bfloat.reshape(sequence_count, span_length, KEY_VALUE_HEADS * HEAD_WIDTH),
            "ctx",
            axis=1,
            tiled=True,
        ),
    )
    key_head_split = gathered_keys.reshape(
        sequence_count, SEQUENCE_LENGTH, KEY_VALUE_HEADS, HEAD_WIDTH
    )
    value_head_split = gathered_values.reshape(
        sequence_count, SEQUENCE_LENGTH, KEY_VALUE_HEADS, HEAD_WIDTH
    )

    def attention_scores():
        raw_scores = (
            jnp.einsum(
                "sqhgd,skhd->shgqk",
                query_groups,
                key_head_split,
                preferred_element_type=jnp.float32,
            )
            * scale_factor
        )
        return jnp.where(permitted_mask, raw_scores, -1e30)

    scores = attention_scores()
    log_total = jax.nn.logsumexp(scores, axis=-1, keepdims=True)
    probs_low = jnp.exp(scores - log_total).astype(jnp.bfloat16)
    attention_output = jnp.einsum(
        "shgqk,skhd->sqhgd", probs_low, value_head_split, preferred_element_type=jnp.float32
    )
    attended_low = attention_output.reshape(count_of_rows, QUERY_HEADS * HEAD_WIDTH).astype(
        jnp.bfloat16
    )
    middle = inputs + jnp.dot(attended_low, mixing_full, preferred_element_type=jnp.float32)
    normed_two = normalized_input(middle, mlp_gain).astype(jnp.bfloat16)
    gate_up = jnp.dot(normed_two, gate_up_full, preferred_element_type=jnp.float32)
    hidden_low = swiglu(gate_up).astype(jnp.bfloat16)
    result = middle + jnp.dot(hidden_low, down_full, preferred_element_type=jnp.float32)
    block_output = result.astype(jnp.bfloat16).reshape(sequence_count, span_length, MODEL_WIDTH)
    query_back, keyval_back, mixing_back, gate_up_back, down_back = (
        query_full,
        keyval_full,
        mixing_full,
        gate_up_full,
        down_full,
    )
    grad_rows = cotangent.reshape(count_of_rows, MODEL_WIDTH)
    down_new = adamw(
        down_weight,
        down_moment,
        down_second,
        owned(hidden_low, grad_rows),
        2.0 / math.sqrt(FF),
        weight_decay,
    )
    hidden_grad = times_transposed(grad_rows, down_back)
    unused_value, swiglu_back = jax.vjp(swiglu, gate_up)
    gate_up_grad = swiglu_back(hidden_grad)[0].astype(jnp.bfloat16)
    gate_up_new = adamw(
        gate_up_weight,
        gate_up_moment,
        gate_up_second,
        owned(normed_two, gate_up_grad),
        2.0 / math.sqrt(MODEL_WIDTH),
        weight_decay,
    )
    normed_two_grad = times_transposed(gate_up_grad, gate_up_back)
    unused_norm, norm_two_back = jax.vjp(normalized_input, middle, mlp_gain)
    middle_part, mlp_gain_grad = norm_two_back(normed_two_grad)
    middle_grad = grad_rows.astype(jnp.float32) + middle_part
    middle_low = middle_grad.astype(jnp.bfloat16)
    mixing_new = adamw(
        mixing_weight,
        mixing_moment,
        mixing_second,
        owned(attended_low, middle_low),
        2.0 / math.sqrt(QUERY_HEADS * HEAD_WIDTH // 32),
        weight_decay,
    )
    attended_grad = (
        times_transposed(middle_low, mixing_back)
        .astype(jnp.bfloat16)
        .reshape(sequence_count, span_length, KEY_VALUE_HEADS, heads_per_group, HEAD_WIDTH)
    )
    scores = attention_scores()
    probs_full = jnp.exp(scores - log_total)
    probs_again = probs_full.astype(jnp.bfloat16)
    prob_grad = jnp.einsum(
        "sqhgd,skhd->shgqk", attended_grad, value_head_split, preferred_element_type=jnp.float32
    )
    row_delta = jnp.sum(probs_full * prob_grad, axis=-1, keepdims=True)
    score_grad = (probs_full * (prob_grad - row_delta)).astype(jnp.bfloat16)
    query_rot_grad = (
        jnp.einsum(
            "shgqk,skhd->sqhgd", score_grad, key_head_split, preferred_element_type=jnp.float32
        )
        * scale_factor
    )
    key_portion = (
        jnp.einsum(
            "shgqk,sqhgd->skhd", score_grad, query_groups, preferred_element_type=jnp.float32
        )
        * scale_factor
    )
    value_portion = jnp.einsum(
        "shgqk,sqhgd->skhd", probs_again, attended_grad, preferred_element_type=jnp.float32
    )
    key_gradient_total, value_gradient_total = (
        lax.psum_scatter(
            key_portion.reshape(sequence_count, SEQUENCE_LENGTH, KEY_VALUE_HEADS * HEAD_WIDTH),
            "ctx",
            scatter_dimension=1,
            tiled=True,
        ),
        lax.psum_scatter(
            value_portion.reshape(sequence_count, SEQUENCE_LENGTH, KEY_VALUE_HEADS * HEAD_WIDTH),
            "ctx",
            scatter_dimension=1,
            tiled=True,
        ),
    )
    unused_heads, heads_back = jax.vjp(
        head_fn, query_raw, key_unnormed, query_gain, key_norm_weight
    )
    query_raw_grad, key_unnormed_gradient, query_gain_grad, key_gain_grad = heads_back(
        (
            query_rot_grad.reshape(sequence_count, span_length, QUERY_HEADS, HEAD_WIDTH),
            key_gradient_total.reshape(sequence_count, span_length, KEY_VALUE_HEADS, HEAD_WIDTH),
        )
    )
    query_grad = query_raw_grad.reshape(count_of_rows, QUERY_HEADS * HEAD_WIDTH).astype(
        jnp.bfloat16
    )
    keyval_grad = jnp.concatenate(
        [
            key_unnormed_gradient.reshape(count_of_rows, KEY_VALUE_HEADS * HEAD_WIDTH),
            value_gradient_total.reshape(count_of_rows, KEY_VALUE_HEADS * HEAD_WIDTH),
        ],
        axis=1,
    ).astype(jnp.bfloat16)
    query_new = adamw(
        query_weight,
        query_moment,
        query_second,
        owned(normed_one, query_grad),
        2.0 / math.sqrt(MODEL_WIDTH),
        weight_decay,
    )
    keyval_new = adamw(
        key_value_weight,
        key_value_first_moment,
        key_value_second_moment,
        owned(normed_one, keyval_grad),
        2.0 / math.sqrt(MODEL_WIDTH),
        weight_decay,
    )
    normed_one_grad = times_transposed(query_grad, query_back) + times_transposed(
        keyval_grad, keyval_back
    )
    unused_first, norm_one_back = jax.vjp(normalized_input, inputs, attn_gain)
    input_part, attn_gain_grad = norm_one_back(normed_one_grad)
    input_grad = (middle_grad + input_part).reshape(sequence_count, span_length, MODEL_WIDTH)
    gain_terms = jnp.concatenate([attn_gain_grad, mlp_gain_grad, query_gain_grad, key_gain_grad])
    gain_total = lax.psum(gain_terms, ("dp", "ctx"))
    gains_new = adamw(norm_gains, gain_moment, gain_second, gain_total, gain_rate, 0.0)
    return (
        block_output,
        input_grad,
        query_new[0],
        query_new[1],
        query_new[2],
        keyval_new[0],
        keyval_new[1],
        keyval_new[2],
        mixing_new[0],
        mixing_new[1],
        mixing_new[2],
        gate_up_new[0],
        gate_up_new[1],
        gate_up_new[2],
        down_new[0],
        down_new[1],
        down_new[2],
        gains_new[0],
        gains_new[1],
        gains_new[2],
    )


def exchange_pairs(count):
    half = count // 2
    first = [(s, 2 * s) for s in range(half)] + [(half + s, 2 * s + 1) for s in range(half)]
    second = [(s, 2 * s + 1) for s in range(half)] + [(half + s, 2 * s) for s in range(half)]
    return first, second


def pair_columns(shard, ctx_index, count):
    half = shard.shape[1] // 2
    low, high = shard[:, :half], shard[:, half:]
    first, second = exchange_pairs(count)
    is_left = ctx_index < count // 2
    got_first = lax.ppermute(jnp.where(is_left, low, high), "ctx", first)
    got_second = lax.ppermute(jnp.where(is_left, high, low), "ctx", second)
    even = ctx_index % 2 == 0
    return jnp.concatenate(
        [jnp.where(even, got_first, got_second), jnp.where(even, got_second, got_first)], axis=1
    )


def unpair_columns(paired, ctx_index, count):
    half = paired.shape[1] // 2
    left, right = paired[:, :half], paired[:, half:]
    first, second = exchange_pairs(count)
    even = ctx_index % 2 == 0
    got_first = lax.ppermute(jnp.where(even, left, right), "ctx", [(b, a) for a, b in first])
    got_second = lax.ppermute(jnp.where(even, right, left), "ctx", [(b, a) for a, b in second])
    is_left = ctx_index < count // 2
    return jnp.concatenate(
        [jnp.where(is_left, got_first, got_second), jnp.where(is_left, got_second, got_first)],
        axis=1,
    )


def gather(values, axis_name):
    return lax.all_gather(values, axis_name, axis=0, tiled=True)


def scatter(values, axis_name):
    return lax.psum_scatter(
        values.astype(jnp.bfloat16), axis_name, scatter_dimension=0, tiled=True
    ).astype(jnp.float32)


def rows_from_all(values, axis_name):
    count = lax.axis_size(axis_name)
    copies = jnp.broadcast_to(values[None], (count,) + values.shape)
    return lax.all_to_all(copies, axis_name, 0, 0).reshape((-1,) + values.shape[1:])


def rows_summed(values, axis_name):
    count = lax.axis_size(axis_name)
    split = values.astype(jnp.bfloat16).reshape((count, -1) + values.shape[1:])
    return jnp.sum(lax.all_to_all(split, axis_name, 0, 0).astype(jnp.float32), axis=0)


def total_over(values, axis_name):
    count = lax.axis_size(axis_name)
    return jnp.sum(rows_from_all(values[None], axis_name).reshape((count,) + values.shape), axis=0)


def attend_kernel(order_ref, start_ref, query_ref, key_ref, value_ref, out_ref, sum_ref):
    block = pl.program_id(0)
    blocks = pl.num_programs(0)
    span = query_ref.shape[0]
    width = HEAD_WIDTH
    factor = HEAD_WIDTH ** (-0.5) * math.log2(math.e)
    query = jnp.concatenate([query_ref[:, :width], query_ref[:, width:]], axis=0)
    own = order_ref[block]
    rows = own * span + lax.broadcasted_iota(jnp.int32, (span, span), 0)
    columns = lax.broadcasted_iota(jnp.int32, (span, span), 1)
    starts = start_ref[...]

    def one_span(turn, total):
        place = pl.multiple_of(order_ref[blocks + turn] * span, span)
        scores = lax.dot_general(
            query,
            key_ref[pl.ds(place, span), :],
            (((1,), (1,)), ((), ())),
            preferred_element_type=jnp.float32,
        )
        at = columns + turn * span
        allowed = (at <= rows) & (at >= starts)
        allowed = jnp.concatenate([allowed, allowed], axis=0)
        terms = jnp.where(allowed, jnp.exp2(scores * factor), 0.0).astype(jnp.bfloat16)
        return total + jnp.dot(
            terms, value_ref[pl.ds(place, span), :], preferred_element_type=jnp.float32
        )

    total = lax.fori_loop(
        order_ref[2 * blocks + block],
        own + 1,
        one_span,
        jnp.zeros((2 * span, 2 * width), jnp.float32),
    )
    mixed = total[:, :width] / total[:, width:]
    out_ref[:, :width] = mixed[:span]
    out_ref[:, width:] = mixed[span:]
    sums = jnp.log2(total[:, width:])
    sum_ref[:, :width] = sums[:span]
    sum_ref[:, width:] = sums[span:]


def attention_forward(query, key, value, order_table, starts):
    length, wide = query.shape
    blocks = order_table.shape[0] // 3
    span = length // blocks
    padded = jnp.concatenate([value, jnp.ones_like(value)], axis=1)
    out, sums = pl.pallas_call(
        attend_kernel,
        grid=(blocks,),
        in_specs=[
            pl.BlockSpec(memory_space=pltpu.SMEM),
            pl.BlockSpec((span, 1), lambda i: (i, 0)),
            pl.BlockSpec((span, wide), lambda i: (i, 0)),
            pl.BlockSpec((length, HEAD_WIDTH), lambda i: (0, 0)),
            pl.BlockSpec((length, 2 * HEAD_WIDTH), lambda i: (0, 0)),
        ],
        out_specs=[
            pl.BlockSpec((span, wide), lambda i: (i, 0)),
            pl.BlockSpec((span, wide), lambda i: (i, 0)),
        ],
        out_shape=[
            jax.ShapeDtypeStruct((length, wide), jnp.float32),
            jax.ShapeDtypeStruct((length, wide), jnp.float32),
        ],
        compiler_params=pltpu.CompilerParams(vmem_limit_bytes=40 * 1024 * 1024),
        cost_estimate=pl.CostEstimate(
            flops=4 * length * length * wide // 2,
            bytes_accessed=12 * length * wide,
            transcendentals=length * length,
        ),
        name="attend",
    )(order_table, starts[:, None], query, key, padded)
    return out, sums[:, ::HEAD_WIDTH]


def attend_back_kernel(
    order_ref,
    start_ref,
    sum_ref,
    delta_ref,
    query_ref,
    grad_ref,
    key_ref,
    value_ref,
    query_grad_ref,
    key_grad_ref,
    value_grad_ref,
):
    block = pl.program_id(0)
    blocks = pl.num_programs(0)
    span = query_ref.shape[0]
    width = HEAD_WIDTH
    scale_factor = HEAD_WIDTH ** (-0.5)
    factor = scale_factor * math.log2(math.e)

    @pl.when(block == 0)
    def _():
        key_grad_ref[...] = jnp.zeros_like(key_grad_ref)
        value_grad_ref[...] = jnp.zeros_like(value_grad_ref)

    query = jnp.concatenate([query_ref[:, :width], query_ref[:, width:]], axis=0)
    grad = jnp.concatenate([grad_ref[:, :width], grad_ref[:, width:]], axis=0)
    own = order_ref[block]
    rows = own * span + lax.broadcasted_iota(jnp.int32, (span, span), 1)
    columns = lax.broadcasted_iota(jnp.int32, (span, span), 0)
    starts = start_ref[0]
    sums = sum_ref[0]
    delta = delta_ref[0]

    def one_span(turn, total):
        place = pl.multiple_of(order_ref[blocks + turn] * span, span)
        here = pl.ds(place, span)
        keys = key_ref[here, :]
        scores = lax.dot_general(
            keys, query, (((1,), (1,)), ((), ())), preferred_element_type=jnp.float32
        )
        prob_grad = lax.dot_general(
            value_ref[here, :], grad, (((1,), (1,)), ((), ())), preferred_element_type=jnp.float32
        )
        at = columns + turn * span
        allowed = (at <= rows) & (at >= starts)
        allowed = jnp.concatenate([allowed, allowed], axis=1)
        probs = jnp.where(allowed, jnp.exp2(scores * factor - sums), 0.0)
        score_grad = (probs * (prob_grad - delta)).astype(jnp.bfloat16)
        value_grad_ref[here, :] += jnp.dot(
            probs.astype(jnp.bfloat16), grad, preferred_element_type=jnp.float32
        )
        key_grad_ref[here, :] += (
            jnp.dot(score_grad, query, preferred_element_type=jnp.float32) * scale_factor
        )
        return total + lax.dot_general(
            score_grad, keys, (((0,), (0,)), ((), ())), preferred_element_type=jnp.float32
        )

    total = lax.fori_loop(
        order_ref[2 * blocks + block],
        own + 1,
        one_span,
        jnp.zeros((2 * span, width), jnp.float32),
    )
    total = total * scale_factor
    query_grad_ref[:, :width] = total[:span]
    query_grad_ref[:, width:] = total[span:]


def attention_backward(query, key, value, order_table, starts, sums, attended, attended_grad):
    length, wide = query.shape
    blocks = order_table.shape[0] // 3
    span = length // blocks
    heads = wide // HEAD_WIDTH
    delta = jnp.sum(
        (attended * attended_grad.astype(jnp.float32)).reshape(length, heads, HEAD_WIDTH), axis=-1
    )

    def along_lanes(columns):
        split = columns.reshape(blocks, span, heads)
        return split.transpose(0, 2, 1).reshape(blocks, 1, heads * span)

    by_block = pl.BlockSpec((span, wide), lambda i: (i, 0))
    whole = pl.BlockSpec((length, HEAD_WIDTH), lambda i: (0, 0))
    lane_row = pl.BlockSpec((1, 1, heads * span), lambda i: (i, 0, 0))
    return pl.pallas_call(
        attend_back_kernel,
        grid=(blocks,),
        in_specs=[
            pl.BlockSpec(memory_space=pltpu.SMEM),
            pl.BlockSpec((1, 1, span), lambda i: (i, 0, 0)),
            lane_row,
            lane_row,
            by_block,
            by_block,
            whole,
            whole,
        ],
        out_specs=[by_block, whole, whole],
        out_shape=[
            jax.ShapeDtypeStruct((length, wide), jnp.float32),
            jax.ShapeDtypeStruct((length, HEAD_WIDTH), jnp.float32),
            jax.ShapeDtypeStruct((length, HEAD_WIDTH), jnp.float32),
        ],
        compiler_params=pltpu.CompilerParams(vmem_limit_bytes=40 * 1024 * 1024),
        cost_estimate=pl.CostEstimate(
            flops=10 * length * length * wide // 2,
            bytes_accessed=16 * length * wide,
            transcendentals=length * length,
        ),
        name="attend_back",
    )(
        order_table,
        starts.reshape(blocks, 1, span),
        along_lanes(sums),
        along_lanes(delta),
        query,
        attended_grad,
        key,
        value,
    )


def span_table(segments, span_order, span_length):
    starts = jnp.sum((segments[None, :] < segments[:, None]).astype(jnp.int32), axis=1)
    blocks = span_order.shape[0]
    block_of = jnp.sum(
        jnp.where(
            span_order[None, :] == jnp.arange(blocks, dtype=jnp.int32)[:, None],
            jnp.arange(blocks, dtype=jnp.int32)[None, :],
            0,
        ),
        axis=1,
    )
    first = jnp.min(starts.reshape(blocks, span_length), axis=1) // span_length
    return starts, jnp.concatenate([span_order, block_of, first]).astype(jnp.int32)


def head_device(
    tokens,
    cotangent,
    segments,
    span_order,
    query_weight,
    query_moment,
    query_second,
    key_value_weight,
    key_value_first_moment,
    key_value_second_moment,
    mixing_weight,
    mixing_moment,
    mixing_second,
    gate_up_weight,
    gate_up_moment,
    gate_up_second,
    down_weight,
    down_moment,
    down_second,
    norm_gains,
    gain_moment,
    gain_second,
):
    span_length = tokens.shape[1]
    count = KEY_VALUE_HEADS
    group = QUERY_HEADS // KEY_VALUE_HEADS
    wide = group * HEAD_WIDTH
    ctx_index = lax.axis_index("ctx")
    attn_gain = norm_gains[:MODEL_WIDTH]
    mlp_gain = norm_gains[MODEL_WIDTH : 2 * MODEL_WIDTH]
    query_gain = norm_gains[2 * MODEL_WIDTH : 2 * MODEL_WIDTH + HEAD_WIDTH]
    key_norm_weight = norm_gains[2 * MODEL_WIDTH + HEAD_WIDTH :]

    tokens_full = gather(tokens[0], "ctx")
    keyval_pair = pair_columns(key_value_weight.astype(jnp.bfloat16), ctx_index, count)
    qkv_weight = rows_from_all(
        jnp.concatenate([query_weight.astype(jnp.bfloat16), keyval_pair], axis=1), "dp"
    )
    mixing_cols = rows_from_all(mixing_weight.astype(jnp.bfloat16), "dp")
    mixing_rows = lax.all_to_all(mixing_cols, "ctx", 0, 1, tiled=True)
    gate_up_cols = rows_from_all(
        pair_columns(gate_up_weight.astype(jnp.bfloat16), ctx_index, count), "dp"
    )
    down_cols = rows_from_all(down_weight.astype(jnp.bfloat16), "dp")
    down_rows = lax.all_to_all(down_cols, "ctx", 0, 1, tiled=True)
    own_cotangent, tokens_full = lax.optimization_barrier((cotangent[0], tokens_full))
    cotangent_full = gather(own_cotangent, "ctx")

    offsets = jnp.arange(SEQUENCE_LENGTH, dtype=jnp.int32) % span_length
    positions = jnp.repeat(span_order[0], span_length) * span_length + offsets
    cosine_table, sine_table = angles_of(positions)
    head_fn = functools.partial(
        head_norms, cosine_table=cosine_table[:, None, :], sine_table=sine_table[:, None, :]
    )

    normed_one = normalized_input(tokens_full.astype(jnp.float32), attn_gain).astype(jnp.bfloat16)
    qkv = jnp.dot(normed_one, qkv_weight, preferred_element_type=jnp.float32)
    query_raw = qkv[:, :wide].reshape(SEQUENCE_LENGTH, group, HEAD_WIDTH)
    key_raw = qkv[:, wide : wide + HEAD_WIDTH].reshape(SEQUENCE_LENGTH, 1, HEAD_WIDTH)
    value = qkv[:, wide + HEAD_WIDTH :].astype(jnp.bfloat16)
    (query_rot, key_rot), heads_back = jax.vjp(
        head_fn, query_raw, key_raw, query_gain, key_norm_weight
    )
    query_rot = query_rot.astype(jnp.bfloat16).reshape(SEQUENCE_LENGTH, wide)
    key_rot = key_rot[:, 0].astype(jnp.bfloat16)
    starts, order_table = span_table(segments[0], span_order[0], span_length)
    attended_wide, sums = attention_forward(query_rot, key_rot, value, order_table, starts)
    attended = attended_wide.astype(jnp.bfloat16)

    inputs = tokens[0].astype(jnp.float32)
    mixed = jnp.dot(attended, mixing_rows, preferred_element_type=jnp.float32).astype(jnp.bfloat16)
    mixed, cotangent_full, gate_up_cols, down_rows = lax.optimization_barrier(
        (mixed, cotangent_full, gate_up_cols, down_rows)
    )
    middle = inputs + scatter(mixed, "ctx")
    normed_two = normalized_input(middle, mlp_gain).astype(jnp.bfloat16)
    normed_two_full = gather(normed_two, "ctx")
    gate_up = jnp.dot(normed_two_full, gate_up_cols, preferred_element_type=jnp.float32)
    half = gate_up.shape[1] // 2

    def gated(both):
        return jax.nn.silu(both[:, :half]) * both[:, half:]

    hidden, gated_back = jax.vjp(gated, gate_up)
    hidden = hidden.astype(jnp.bfloat16)
    hidden_grad = times_transposed(cotangent_full, down_rows)
    gate_up_grad = gated_back(hidden_grad)[0].astype(jnp.bfloat16)
    normed_two_grad = scatter(times_transposed(gate_up_grad, gate_up_cols), "ctx")
    unused_norm, norm_two_back = jax.vjp(normalized_input, middle, mlp_gain)
    middle_part, mlp_gain_grad = norm_two_back(normed_two_grad)
    middle_grad = cotangent[0].astype(jnp.float32) + middle_part
    middle_low = gather(middle_grad.astype(jnp.bfloat16), "ctx")
    hidden_out = jnp.dot(hidden, down_rows, preferred_element_type=jnp.float32)
    hidden_out, middle_low = lax.optimization_barrier(
        (hidden_out.astype(jnp.bfloat16), middle_low)
    )
    hidden_sum = scatter(hidden_out, "ctx")
    attended_grad = times_transposed(middle_low, mixing_rows).astype(jnp.bfloat16)

    def rows_back(gradient):
        columns = lax.all_to_all(gradient.astype(jnp.bfloat16), "ctx", 1, 0, tiled=True)
        return rows_summed(columns, "dp")

    down_total = rows_back(rows_product(hidden, cotangent_full))
    gate_up_total = unpair_columns(
        rows_summed(rows_product(normed_two_full, gate_up_grad), "dp").astype(jnp.bfloat16),
        ctx_index,
        count,
    ).astype(jnp.float32)
    mixing_total = rows_back(rows_product(attended, middle_low))

    query_rot_grad, key_rot_grad, value_grad = attention_backward(
        query_rot, key_rot, value, order_table, starts, sums, attended_wide, attended_grad
    )
    query_raw_grad, key_raw_grad, query_gain_grad, key_gain_grad = heads_back(
        (
            query_rot_grad.reshape(SEQUENCE_LENGTH, group, HEAD_WIDTH),
            key_rot_grad[:, None, :],
        )
    )
    qkv_grad = jnp.concatenate(
        [query_raw_grad.reshape(SEQUENCE_LENGTH, wide), key_raw_grad[:, 0], value_grad], axis=1
    ).astype(jnp.bfloat16)
    normed_one_part = times_transposed(qkv_grad, qkv_weight)
    attn_gain_grad = jax.vjp(
        lambda gain: normalized_input(tokens_full.astype(jnp.float32), gain), attn_gain
    )[1](normed_one_part)[0]
    normed_one_low, hidden_sum = lax.optimization_barrier(
        (normed_one_part.astype(jnp.bfloat16), hidden_sum)
    )
    block_output = (middle + hidden_sum).astype(jnp.bfloat16)[None]
    normed_one_grad = scatter(normed_one_low, "ctx")
    qkv_total = rows_summed(rows_product(normed_one, qkv_grad), "dp").astype(jnp.bfloat16)
    query_total = qkv_total[:, :wide].astype(jnp.float32)
    keyval_total = unpair_columns(qkv_total[:, wide:], ctx_index, count).astype(jnp.float32)
    unused_first, norm_one_back = jax.vjp(normalized_input, inputs, attn_gain)
    input_part = norm_one_back(normed_one_grad)[0]
    input_grad = (middle_grad + input_part)[None]

    gain_terms = jnp.concatenate([attn_gain_grad, mlp_gain_grad, query_gain_grad, key_gain_grad])
    gain_total = total_over(total_over(gain_terms, "ctx"), "dp")
    model_rate = 2.0 / math.sqrt(MODEL_WIDTH)
    mixing_rate = 2.0 / math.sqrt(QUERY_HEADS * HEAD_WIDTH // 32)
    down_rate = 2.0 / math.sqrt(FF)
    return (
        block_output,
        input_grad,
        *adamw(query_weight, query_moment, query_second, query_total, model_rate, weight_decay),
        *adamw(
            key_value_weight,
            key_value_first_moment,
            key_value_second_moment,
            keyval_total,
            model_rate,
            weight_decay,
        ),
        *adamw(
            mixing_weight, mixing_moment, mixing_second, mixing_total, mixing_rate, weight_decay
        ),
        *adamw(
            gate_up_weight, gate_up_moment, gate_up_second, gate_up_total, model_rate, weight_decay
        ),
        *adamw(down_weight, down_moment, down_second, down_total, down_rate, weight_decay),
        *adamw(norm_gains, gain_moment, gain_second, gain_total, gain_rate, 0.0),
    )


def solution(mesh):
    in_specs = (
        P("dp", "ctx", None),
        P("dp", "ctx", None),
        P("dp", None),
        P("dp", None),
        P("dp", "ctx"),
        P("dp", "ctx"),
        P("dp", "ctx"),
        P("dp", "ctx"),
        P("dp", "ctx"),
        P("dp", "ctx"),
        P("dp", "ctx"),
        P("dp", "ctx"),
        P("dp", "ctx"),
        P("dp", "ctx"),
        P("dp", "ctx"),
        P("dp", "ctx"),
        P("dp", "ctx"),
        P("dp", "ctx"),
        P("dp", "ctx"),
        P(),
        P(),
        P(),
    )
    out_specs = (
        P("dp", "ctx", None),
        P("dp", "ctx", None),
        P("dp", "ctx"),
        P("dp", "ctx"),
        P("dp", "ctx"),
        P("dp", "ctx"),
        P("dp", "ctx"),
        P("dp", "ctx"),
        P("dp", "ctx"),
        P("dp", "ctx"),
        P("dp", "ctx"),
        P("dp", "ctx"),
        P("dp", "ctx"),
        P("dp", "ctx"),
        P("dp", "ctx"),
        P("dp", "ctx"),
        P("dp", "ctx"),
        P(),
        P(),
        P(),
    )
    fits = mesh.shape["ctx"] == KEY_VALUE_HEADS and mesh.shape["dp"] == SEQUENCES
    per_device = head_device if fits else wide_device
    return jax.shard_map(
        per_device, mesh=mesh, in_specs=in_specs, out_specs=out_specs, check_vma=False
    )
```
